32 devices in a mesh: ctx: 2 (over y), exp: 4 (over z), ffn: 4 (over x, core).
Axes of the slice: x: 2, y: 2, z: 4, core: 2. Of those that a mesh axis runs over, the one named last changes fastest.
Arguments:
- query_rows: bfloat16 [1024, 4096], P('ctx', ('exp', 'ffn')), may hold values from -6 to 6
- key_rows: bfloat16 [1024, 1024], P('ctx', 'exp'), may hold values from -6 to 6
- value_rows: bfloat16 [1024, 1024], P('ctx', 'exp'), may hold values from -6 to 6
- head_output: bfloat16 [1024, 4096], P('ctx', ('exp', 'ffn')), may hold values from -6 to 6
- output_grad: bfloat16 [1024, 4096], P('ctx', ('exp', 'ffn')), may hold values from -6 to 6
- row_logsumexp: float32 [32, 1024], P(('exp', 'ffn'), 'ctx'), as said below
- token_rows: bfloat16 [1024, 4096], P(('exp', 'ffn'), 'ctx'), may hold values from -6 to 6
- token_grad: bfloat16 [1024, 4096], P(('exp', 'ffn'), 'ctx'), may hold values from -6 to 6
- gate_probs: float32 [1024, 2], P(('exp', 'ffn')), may hold values from 0.05 to 0.95
- expert_ids: int32 [1024, 2], P(('exp', 'ffn')), may hold values from 0 to 3, all different within a row; in each aligned block of 64 rows (0 to 63, 64 to 127, ...) at most 33 rows name the same one
- w_gate: bfloat16 [4, 4096, 7168], P('exp', 'ctx', 'ffn'), may hold values from -0.09375 to 0.09375
- w_up: bfloat16 [4, 4096, 7168], P('exp', 'ctx', 'ffn'), may hold values from -0.09375 to 0.09375
- w_down: bfloat16 [4, 7168, 4096], P('exp', 'ffn', 'ctx'), may hold values from -0.0625 to 0.0625
Outputs:
- query_grad: bfloat16 [1024, 4096], P('ctx', ('exp', 'ffn'))
- key_grad: bfloat16 [1024, 1024], P(('ctx', 'ffn'), 'exp')
- value_grad: bfloat16 [1024, 1024], P(('ctx', 'ffn'), 'exp')
- input_grad: bfloat16 [1024, 4096], P(('exp', 'ffn'), 'ctx')
- gate_grad: bfloat16 [4, 4096, 7168], P('exp', 'ctx', 'ffn')
- up_grad: bfloat16 [4, 4096, 7168], P('exp', 'ctx', 'ffn')
The draws below stay inside these ranges and needn't reach their ends.
Inputs may be any that keep to these rules, and one draw needn't show every extreme that they name: `expert_ids`: each token names 2 different experts. In the rows of one device (aligned blocks of 64 tokens) no expert is named by more than 33 routes, and in every draw some block has an expert named by exactly 33 routes. row_logsumexp[h, i] is the log of the sum over j <= i of exp(128^-0.5 query_rows_h[i] . key_rows_kv[j]), with the bfloat16 values of both.
All inputs are finite; a program needn't handle non-finite values.
Results may differ from the reference program's by a relative error of at most 0.015.
Values may be sent and summed in bfloat16 or wider, within the bound.
A program may use at most 128 MiB of HBM per device.

```python
import math
import jax
import jax.numpy as jnp
import numpy as np
from jax import lax

D = 4096
QH = 32
KVH = 8
HEAD = 128
TOP = 2
FF = 7168
TOK_DEV = 64
EXPERTS = 4
TOKENS = 1024
SLOT = 33
N_CTX = 2


def query_values(key):
    drawn = jax.random.truncated_normal(jax.random.fold_in(key, 501), -6.0, 6.0, (TOKENS, QH * HEAD), jnp.float32)
    return drawn.astype(jnp.bfloat16)


def key_values(key):
    drawn = jax.random.truncated_normal(jax.random.fold_in(key, 502), -6.0, 6.0, (TOKENS, KVH * HEAD), jnp.float32)
    return drawn.astype(jnp.bfloat16)


def draw_query_rows(key, part):
    return query_values(key)


def draw_key_rows(key, part):
    return key_values(key)


def draw_row_logsumexp(key, part):
    queries = query_values(key).astype(jnp.float32)
    keyset = key_values(key).astype(jnp.float32)
    group_size = QH // KVH
    score_scale = HEAD ** (-0.5)
    position = jnp.arange(TOKENS, dtype=jnp.int32)
    allowed = position[None, :] <= position[:, None]

    def one_head(head_id):
        query_head = lax.dynamic_slice_in_dim(queries, head_id * HEAD, HEAD, 1)
        key_head = lax.dynamic_slice_in_dim(keyset, head_id // group_size * HEAD, HEAD, 1)
        scores = jnp.dot(query_head, key_head.T, precision=lax.Precision.HIGHEST) * score_scale
        scores = jnp.where(allowed, scores, -jnp.inf)
        return jax.nn.logsumexp(scores, axis=1)
    return lax.map(one_head, jnp.arange(QH, dtype=jnp.int32)).astype(jnp.float32)


def steps_of(own_key, extent, shards, low, largest):
    def one(dim, parts):
        steps = jax.random.uniform(jax.random.fold_in(jax.random.fold_in(own_key, 6), dim), (parts,), jnp.float32, low / len(shards), largest / len(shards))
        return jnp.repeat(jnp.exp(steps), extent[dim] // parts).reshape((-1,) + (1,) * (len(extent) - dim - 1))

    gain = one(*shards[0])
    for cut in shards[1:]:
        gain = gain * one(*cut)
    return gain


def deal_out(key, own, number, rows, amount, top, most, lean):
    sequence = jax.random.permutation(key, amount)
    heavy_load, ordinary = shares(amount, rows * top, most, lean, True), shares(amount, rows * top, most, lean, False)
    places = jnp.arange(amount)

    def named(sizes, offset_by):
        used = int((sizes > 0).sum())
        fixed = max(1, used // 4)
        moved = fixed + (places - fixed + offset_by * (used - fixed)) % max(1, amount - fixed)
        return jnp.zeros((amount,), jnp.int32).at[sequence[jnp.where(places < fixed, places, moved)]].set(jnp.asarray(sizes, jnp.int32))

    sizes = jnp.where(number % 4 == 0, named(heavy_load, number // 4), named(ordinary, number - number // 4 - 1))
    mixed = jax.random.permutation(jax.random.fold_in(own, 3), amount)
    giver, receiver = mixed[0:amount // 2 * 2:2], mixed[1:amount // 2 * 2:2]
    room = jnp.minimum(sizes[giver] - 1, most - sizes[receiver]) // 2
    room = jnp.where((giver == sequence[0]) | (receiver == sequence[0]) | (sizes[receiver] == 0), 0, jnp.maximum(room, 0))
    moved = jax.random.randint(jax.random.fold_in(own, 4), (amount // 2,), 0, 1 << 20) % (room + 1)
    sizes = sizes.at[giver].add(-moved).at[receiver].add(moved)
    labels = jnp.searchsorted(jnp.cumsum(sizes), jnp.arange(rows * top), side="right").astype(jnp.int32)
    listing = labels.reshape(top, rows).T
    listing = listing[jax.random.permutation(jax.random.fold_in(own, 1), rows)]
    offset_by = jax.random.randint(jax.random.fold_in(own, 2), (rows, 1), 0, top)
    return jnp.take_along_axis(listing, (jnp.arange(top)[None, :] + offset_by) % top, axis=1)


def shares(count, total, limit, slope, full):
    portions = [(1 << 20) // math.isqrt(rank ** slope) + 1 for rank in range(1, count + 1)]
    largest = limit if full else min(limit, max(-(-total // count), total * portions[0] // sum(portions)))
    least = 1 if total - largest >= count - 1 else 0
    given, spare = [largest] + [least] * (count - 1), total - largest - least * (count - 1)
    while spare > 0:
        free = [i for i in range(1, count) if given[i] < largest] or [i for i in range(1, count) if given[i] < limit]
        whole, remaining = sum([portions[i] for i in free]), spare
        for i in free:
            addition = min(limit - given[i], max(1, remaining * portions[i] // whole), spare)
            given[i] = given[i] + addition
            spare = spare - addition
    return np.array(given)


def scatter_about(stream_key, dims, spread, bound, pieces=(), kind=jnp.bfloat16):
    array = spread * jax.random.normal(stream_key, dims, jnp.float32)
    if pieces:
        array = array * steps_of(stream_key, dims, pieces, -0.22, 0.18)
    return jnp.clip(array, -bound, bound).astype(kind)


def setup_inputs(seed: int = 0) -> dict:
    streams_of = jax.random.split(jax.random.key(seed), 14)
    query_rows = draw_query_rows(jax.random.fold_in(streams_of[13], 71), 0)
    key_rows = draw_key_rows(jax.random.fold_in(streams_of[13], 71), 0)
    value_rows = scatter_about(streams_of[2], (TOKENS, KVH * HEAD), 1.0, 6.0, ((0, 2), (1, 4)))
    head_output = scatter_about(streams_of[3], (TOKENS, QH * HEAD), 0.5, 6.0, ((0, 2), (1, 16)))
    output_grad = scatter_about(streams_of[4], (TOKENS, QH * HEAD), 1.0, 6.0, ((0, 2), (1, 16)))
    row_logsumexp = draw_row_logsumexp(jax.random.fold_in(streams_of[13], 71), 0)
    token_rows = scatter_about(streams_of[6], (TOKENS, D), 1.0, 6.0, ((0, 16), (1, 2)))
    token_grad = scatter_about(streams_of[7], (TOKENS, D), 1.0, 6.0, ((0, 16), (1, 2)))
    gate_probs = jnp.clip(0.05 + 0.9 * jax.random.uniform(streams_of[8], (TOKENS, TOP), jnp.float32) ** steps_of(streams_of[8], (TOKENS, TOP), ((0, 16),), -0.2, 0.2), 0.05, 0.95)
    expert_ids_keys = jax.random.split(jax.random.fold_in(streams_of[9], 1), TOKENS // TOK_DEV)
    expert_ids_turns = jax.random.permutation(jax.random.fold_in(streams_of[9], 3), TOKENS // TOK_DEV)
    expert_ids = jax.vmap(lambda own, number: deal_out(jax.random.fold_in(streams_of[9], 2), own, number, TOK_DEV, EXPERTS, TOP, SLOT, 2))(expert_ids_keys, expert_ids_turns).reshape((TOKENS, TOP))
    w_gate = scatter_about(streams_of[10], (EXPERTS, D, FF), D ** -0.5, 0.09375, ((0, 4), (1, 2), (2, 4)))
    w_up = scatter_about(streams_of[11], (EXPERTS, D, FF), D ** -0.5, 0.09375, ((0, 4), (1, 2), (2, 4)))
    w_down = scatter_about(streams_of[12], (EXPERTS, FF, D), FF ** -0.5, 0.0625, ((0, 4), (1, 4), (2, 2)))
    return {"query_rows": query_rows, "key_rows": key_rows, "value_rows": value_rows, "head_output": head_output, "output_grad": output_grad, "row_logsumexp": row_logsumexp, "token_rows": token_rows, "token_grad": token_grad, "gate_probs": gate_probs, "expert_ids": expert_ids, "w_gate": w_gate, "w_up": w_up, "w_down": w_down}


def block_sums(row_block, weight):
    feat_width = D // N_CTX

    def step(running, block_id):
        partial_value = jnp.dot(lax.dynamic_slice_in_dim(row_block, block_id * feat_width, feat_width, 1),
                          lax.dynamic_slice_in_dim(weight, block_id * feat_width, feat_width, 0),
                          preferred_element_type=jnp.float32)
        partial_value = lax.optimization_barrier(partial_value.astype(jnp.bfloat16))
        return running + partial_value.astype(jnp.float32), None

    running, unused = lax.scan(step, jnp.zeros((row_block.shape[0], weight.shape[1]), jnp.float32),
                               jnp.arange(N_CTX, dtype=jnp.int32))
    return running


def attention_grads(query_rows, key_rows, value_rows, head_output, output_grad, row_logsumexp):
    group_size = QH // KVH
    score_scale = HEAD ** -0.5
    position = jnp.arange(TOKENS, dtype=jnp.int32)
    allowed = position[None, :] <= position[:, None]

    def one_head(head_id):
        kv_column = (head_id // group_size) * HEAD
        query_head = lax.dynamic_slice_in_dim(query_rows, head_id * HEAD, HEAD, 1)
        key_head = lax.dynamic_slice_in_dim(key_rows, kv_column, HEAD, 1)
        value_head = lax.dynamic_slice_in_dim(value_rows, kv_column, HEAD, 1)
        out_head = lax.dynamic_slice_in_dim(head_output, head_id * HEAD, HEAD, 1)
        grad_head = lax.dynamic_slice_in_dim(output_grad, head_id * HEAD, HEAD, 1)
        row_delta = jnp.sum(out_head.astype(jnp.float32) * grad_head.astype(jnp.float32), axis=1)
        scores = jnp.dot(query_head, key_head.T, preferred_element_type=jnp.float32) * score_scale
        probabilities = jnp.where(allowed, jnp.exp(scores - row_logsumexp[head_id][:, None]), 0.0)
        probs_low = probabilities.astype(jnp.bfloat16)
        value_part = jnp.dot(probs_low.T, grad_head, preferred_element_type=jnp.float32)
        dprob = jnp.dot(grad_head, value_head.T, preferred_element_type=jnp.float32)
        dscores = (probabilities * (dprob - row_delta[:, None])).astype(jnp.bfloat16)
        query_part = jnp.dot(dscores, key_head, preferred_element_type=jnp.float32)
        key_part = jnp.dot(dscores.T, query_head, preferred_element_type=jnp.float32)
        return query_part, key_part, value_part

    query_part, key_part, value_part = lax.map(one_head, jnp.arange(QH, dtype=jnp.int32))
    query_grad = (score_scale * query_part).transpose(1, 0, 2).reshape(TOKENS, QH * HEAD).astype(jnp.bfloat16)
    key_sum = jnp.sum(key_part.reshape(KVH, group_size, TOKENS, HEAD), axis=1)
    value_sum = jnp.sum(value_part.reshape(KVH, group_size, TOKENS, HEAD), axis=1)
    key_grad = (score_scale * key_sum).transpose(1, 0, 2).reshape(TOKENS, KVH * HEAD).astype(jnp.bfloat16)
    value_grad = value_sum.transpose(1, 0, 2).reshape(TOKENS, KVH * HEAD).astype(jnp.bfloat16)
    return query_grad, key_grad, value_grad


def expert_grads(token_rows, token_grad, gate_probs, expert_ids, w_gate, w_up, w_down):
    blocks = TOKENS // TOK_DEV
    per_block = TOK_DEV * TOP
    routes = expert_ids.reshape(blocks, per_block)
    onehot = (routes[:, :, None] == jnp.arange(EXPERTS, dtype=jnp.int32)[None, None, :]).astype(jnp.int32)
    position = jnp.sum((jnp.cumsum(onehot, axis=1) - 1) * onehot, axis=2)
    route_index = jnp.arange(TOKENS * TOP, dtype=jnp.int32).reshape(blocks, per_block)
    block_index = jnp.broadcast_to(jnp.arange(blocks, dtype=jnp.int32)[:, None], (blocks, per_block))
    slot_table = jnp.full((EXPERTS, blocks, SLOT), TOKENS * TOP, jnp.int32)
    slot_table = slot_table.at[routes, block_index, position].set(route_index)
    slot_table = slot_table.reshape(EXPERTS, blocks * SLOT)
    repeated_grad = jnp.repeat(token_grad, TOP, axis=0).astype(jnp.float32)
    scaled = (gate_probs.reshape(-1, 1) * repeated_grad).astype(jnp.bfloat16)
    padded_grad = jnp.concatenate([scaled, jnp.zeros((1, D), jnp.bfloat16)], axis=0)
    padded_rows = jnp.concatenate([jnp.repeat(token_rows, TOP, axis=0), jnp.zeros((1, D), jnp.bfloat16)], axis=0)

    def one_expert(inputs):
        picked, gate_w, up_w, down_w = inputs
        rows_x = padded_rows[picked]
        rows_dy = padded_grad[picked]
        gate_sum = block_sums(rows_x, gate_w)
        up_sum = block_sums(rows_x, up_w)
        hidden = block_sums(rows_dy, down_w.T)
        sigmoid_gate = jax.nn.sigmoid(gate_sum)
        gate_low = (hidden * up_sum * sigmoid_gate * (1.0 + gate_sum * (1.0 - sigmoid_gate))).astype(jnp.bfloat16)
        up_low = (hidden * gate_sum * sigmoid_gate).astype(jnp.bfloat16)
        gate_part = jnp.dot(rows_x.T, gate_low, preferred_element_type=jnp.float32).astype(jnp.bfloat16)
        up_part = jnp.dot(rows_x.T, up_low, preferred_element_type=jnp.float32).astype(jnp.bfloat16)
        route_part = (jnp.dot(gate_low, gate_w.T, preferred_element_type=jnp.float32)
                      + jnp.dot(up_low, up_w.T, preferred_element_type=jnp.float32))
        return gate_part, up_part, route_part

    gate_grad, up_grad, route_part = lax.map(one_expert, (slot_table, w_gate, w_up, w_down))
    summed = jnp.zeros((TOKENS * TOP + 1, D), jnp.float32).at[slot_table.reshape(-1)].add(route_part.reshape(-1, D))
    input_grad = jnp.sum(summed[:TOKENS * TOP].reshape(TOKENS, TOP, D), axis=1).astype(jnp.bfloat16)
    return input_grad, gate_grad, up_grad


def reference(query_rows, key_rows, value_rows, head_output, output_grad, row_logsumexp,
              token_rows, token_grad, gate_probs, expert_ids, w_gate, w_up, w_down):
    query_grad, key_grad, value_grad = attention_grads(query_rows, key_rows, value_rows,
                                                       head_output, output_grad, row_logsumexp)
    input_grad, gate_grad, up_grad = expert_grads(token_rows, token_grad, gate_probs, expert_ids,
                                                  w_gate, w_up, w_down)
    return query_grad, key_grad, value_grad, input_grad, gate_grad, up_grad
```

```python
import jax
import jax.numpy as jnp
from jax import lax
from jax.sharding import PartitionSpec as P

QH = 32
KVH = 8
HEAD = 128
TOP = 2
EXP_DEV = 1
TOK_DEV = 64


def attention_part(query_rows, key_rows, value_rows, head_output, output_grad, row_logsumexp):
    tok_ctx = query_rows.shape[0]
    q_heads = query_rows.shape[1] // HEAD
    kv_heads = key_rows.shape[1] // HEAD
    group_size = QH // KVH
    score_scale = HEAD ** (-0.5)
    ffn_index = lax.axis_index("ffn")
    ctx_index = lax.axis_index("ctx")
    query_pos = ctx_index * tok_ctx + jnp.arange(tok_ctx, dtype=jnp.int32)
    product = head_output.astype(jnp.float32) * output_grad.astype(jnp.float32)
    row_delta = jnp.sum(product.reshape(tok_ctx, q_heads, HEAD), axis=2)
    all_keys = tok_ctx * lax.axis_size("ctx")
    contract_rows = (((0,), (0,)), ((), ()))
    contract_cols = (((1,), (1,)), ((), ()))
    start_state = (
        jnp.zeros((tok_ctx, q_heads * HEAD), jnp.float32),
        jnp.zeros((all_keys, kv_heads * HEAD), jnp.float32),
        jnp.zeros((all_keys, kv_heads * HEAD), jnp.float32),
    )
    first_row = jnp.int32(0)
    key_block = lax.all_gather(key_rows, "ctx", axis=0, tiled=True)
    value_block = lax.all_gather(value_rows, "ctx", axis=0, tiled=True)
    key_count = key_block.shape[0]
    key_pos = jnp.arange(key_count, dtype=jnp.int32)
    allowed = key_pos[None, :] <= query_pos[:, None]

    def head_step(head_id, state):
        dq_acc, dk_acc, dv_acc = state
        kv_column = (ffn_index * q_heads + head_id) // group_size * HEAD
        key_head = lax.dynamic_slice_in_dim(key_block, kv_column, HEAD, 1)
        value_head = lax.dynamic_slice_in_dim(value_block, kv_column, HEAD, 1)
        query_head = lax.dynamic_slice_in_dim(query_rows, head_id * HEAD, HEAD, 1)
        grad_head = lax.dynamic_slice_in_dim(output_grad, head_id * HEAD, HEAD, 1)
        lse_row = lax.dynamic_index_in_dim(row_logsumexp, head_id, 0, False)
        delta_row = lax.dynamic_index_in_dim(row_delta, head_id, 1, False)
        scores = (
            lax.dot_general(query_head, key_head, contract_cols, preferred_element_type=jnp.float32)
            * score_scale
        )
        probabilities = jnp.where(allowed, jnp.exp(scores - lse_row[:, None]), 0.0)
        dprob = lax.dot_general(
            grad_head, value_head, contract_cols, preferred_element_type=jnp.float32
        )
        dscores = (probabilities * (dprob - delta_row[:, None])).astype(jnp.bfloat16)
        dq_add = jnp.dot(dscores, key_head, preferred_element_type=jnp.float32)
        old_q = lax.dynamic_slice_in_dim(dq_acc, head_id * HEAD, HEAD, 1)
        dq_acc = lax.dynamic_update_slice_in_dim(dq_acc, old_q + dq_add, head_id * HEAD, 1)
        probs_low = probabilities.astype(jnp.bfloat16)
        value_add = lax.dot_general(
            probs_low, grad_head, contract_rows, preferred_element_type=jnp.float32
        )
        key_add = lax.dot_general(
            dscores, query_head, contract_rows, preferred_element_type=jnp.float32
        )
        old_key = lax.dynamic_slice(dk_acc, (first_row, kv_column), (key_count, HEAD))
        dk_acc = lax.dynamic_update_slice(dk_acc, old_key + key_add, (first_row, kv_column))
        old_value = lax.dynamic_slice(dv_acc, (first_row, kv_column), (key_count, HEAD))
        dv_acc = lax.dynamic_update_slice(dv_acc, old_value + value_add, (first_row, kv_column))
        return (dq_acc, dk_acc, dv_acc)

    finals = lax.fori_loop(0, q_heads, head_step, start_state)
    query_grad = (score_scale * finals[0]).astype(jnp.bfloat16)
    key_sum, value_sum = (
        lax.psum_scatter(finals[1], ("ctx", "ffn"), scatter_dimension=0, tiled=True),
        lax.psum_scatter(finals[2], ("ctx", "ffn"), scatter_dimension=0, tiled=True),
    )
    return (
        query_grad,
        (score_scale * key_sum).astype(jnp.bfloat16),
        value_sum.astype(jnp.bfloat16),
    )


def local_grads(gate_sum, up_sum, hidden):
    sigmoid_gate = jax.nn.sigmoid(gate_sum)
    gate_low = (hidden * up_sum * sigmoid_gate * (1.0 + gate_sum * (1.0 - sigmoid_gate))).astype(
        jnp.bfloat16
    )
    up_low = (hidden * gate_sum * sigmoid_gate).astype(jnp.bfloat16)
    return (gate_low, up_low)


def expert_part(token_rows, token_grad, gate_probs, expert_ids, w_gate, w_up, w_down):
    experts = EXP_DEV * lax.axis_size("exp")
    copies = lax.axis_size("ffn")
    slot_count = min(TOK_DEV, TOK_DEV * TOP // experts + 1)
    tokens_here = token_rows.shape[0]
    feat_width = token_rows.shape[1]
    flat_ids = expert_ids.reshape(-1)
    onehot = (flat_ids[:, None] == jnp.arange(experts, dtype=jnp.int32)[None, :]).astype(jnp.int32)
    position = jnp.sum((jnp.cumsum(onehot, axis=0) - 1) * onehot, axis=1)
    target = flat_ids * slot_count + position
    placing = (
        jnp.arange(experts * slot_count, dtype=jnp.int32)[:, None] == target[None, :]
    ).astype(jnp.float32)
    token_pick = placing.reshape(experts * slot_count, tokens_here, TOP)
    pick_rows = jnp.sum(token_pick, axis=2)
    pick_scaled = jnp.sum(token_pick * gate_probs[None, :, :], axis=2)
    sent_rows = jnp.dot(
        pick_rows.astype(jnp.bfloat16), token_rows, preferred_element_type=jnp.float32
    ).astype(jnp.bfloat16)
    sent_grad = jnp.dot(
        pick_scaled, token_grad.astype(jnp.float32), precision=lax.Precision.HIGHEST
    ).astype(jnp.bfloat16)

    def spread(block):
        widened = jnp.broadcast_to(
            block.reshape(experts, 1, slot_count, feat_width),
            (experts, copies, slot_count, feat_width),
        )
        return widened.reshape(experts * copies * slot_count, feat_width)

    rows_x, rows_dy = (
        lax.all_to_all(spread(sent_rows), ("exp", "ffn"), split_axis=0, concat_axis=0, tiled=True),
        lax.all_to_all(spread(sent_grad), ("exp", "ffn"), split_axis=0, concat_axis=0, tiled=True),
    )
    gate_w = w_gate[0]
    up_w = w_up[0]
    down_w = w_down[0]
    contract_rows = (((0,), (0,)), ((), ()))
    contract_cols = (((1,), (1,)), ((), ()))
    gate_part = jnp.dot(rows_x, gate_w, preferred_element_type=jnp.float32)
    up_part = jnp.dot(rows_x, up_w, preferred_element_type=jnp.float32)
    hidden_part = lax.dot_general(
        rows_dy, down_w, contract_cols, preferred_element_type=jnp.float32
    )
    gate_sum, up_sum, hidden = (
        lax.psum(gate_part.astype(jnp.bfloat16), "ctx").astype(jnp.float32),
        lax.psum(up_part.astype(jnp.bfloat16), "ctx").astype(jnp.float32),
        lax.psum(hidden_part.astype(jnp.bfloat16), "ctx").astype(jnp.float32),
    )
    gate_low, up_low = local_grads(gate_sum, up_sum, hidden)
    gate_grad = lax.dot_general(rows_x, gate_low, contract_rows, preferred_element_type=jnp.float32)
    up_grad = lax.dot_general(rows_x, up_low, contract_rows, preferred_element_type=jnp.float32)
    route_part = lax.dot_general(
        gate_low, gate_w, contract_cols, preferred_element_type=jnp.float32
    ) + lax.dot_general(up_low, up_w, contract_cols, preferred_element_type=jnp.float32)
    returned = lax.all_to_all(
        route_part.astype(jnp.bfloat16), ("exp", "ffn"), split_axis=0, concat_axis=0, tiled=True
    ).astype(route_part.dtype)
    route_grad = jnp.sum(returned.reshape(experts, copies, slot_count, feat_width), axis=1)
    route_grad = route_grad.reshape(experts * slot_count, feat_width)
    input_grad = lax.dot_general(
        pick_rows,
        route_grad,
        contract_rows,
        precision=lax.Precision.HIGHEST,
        preferred_element_type=jnp.float32,
    ).astype(jnp.bfloat16)
    return (input_grad, gate_grad.astype(jnp.bfloat16)[None], up_grad.astype(jnp.bfloat16)[None])


def swap(block, axis, mask):
    size = lax.axis_size(axis)
    return lax.ppermute(block, axis, [(i, i ^ mask) for i in range(size)])


def shift(block, axis, step):
    size = lax.axis_size(axis)
    return lax.ppermute(block, axis, [(i, (i + step) % size) for i in range(size)])


ROWS_ROWS = (((0,), (0,)), ((), ()))
COLS_COLS = (((1,), (1,)), ((), ()))


def attention_pair(query_rows, key_rows, value_rows, head_output, output_grad, row_logsumexp):
    rows = query_rows.shape[0]
    q_heads = query_rows.shape[1] // HEAD
    score_scale = HEAD ** (-0.5)
    ffn_index = lax.axis_index("ffn")
    late = lax.axis_index("ctx") == 1
    kv_first = ffn_index < 2
    odd = ffn_index % 2 == 1
    key_own = jnp.where(kv_first, key_rows[:, :HEAD], key_rows[:, HEAD:])
    value_own = jnp.where(kv_first, value_rows[:, :HEAD], value_rows[:, HEAD:])
    sent = lax.ppermute(jnp.concatenate([key_own, value_own], axis=1), "ctx", [(0, 1)])
    key_old, value_old = sent[:, :HEAD], sent[:, HEAD:]
    product = head_output.astype(jnp.float32) * output_grad.astype(jnp.float32)
    row_delta = jnp.sum(product.reshape(rows, q_heads, HEAD), axis=2)
    place = jnp.arange(rows, dtype=jnp.int32)
    causal = place[None, :] <= place[:, None]
    before = jnp.broadcast_to(late, (rows, rows))
    query_parts = []
    own_sum = old_sum = 0.0
    for head in range(q_heads):
        query_head = query_rows[:, head * HEAD : (head + 1) * HEAD]
        grad_head = output_grad[:, head * HEAD : (head + 1) * HEAD]
        lse = row_logsumexp[head][:, None]
        delta = row_delta[:, head][:, None]

        def against(keys, values, allowed):
            scores = (
                lax.dot_general(query_head, keys, COLS_COLS, preferred_element_type=jnp.float32)
                * score_scale
            )
            probs = jnp.where(allowed, jnp.exp(scores - lse), 0.0)
            dprob = lax.dot_general(
                grad_head, values, COLS_COLS, preferred_element_type=jnp.float32
            )
            dscores = (probs * (dprob - delta)).astype(jnp.bfloat16)
            dq = jnp.dot(dscores, keys, preferred_element_type=jnp.float32)
            dk = lax.dot_general(
                dscores, query_head, ROWS_ROWS, preferred_element_type=jnp.float32
            )
            dv = lax.dot_general(
                probs.astype(jnp.bfloat16), grad_head, ROWS_ROWS, preferred_element_type=jnp.float32
            )
            return dq, jnp.concatenate([dk, dv], axis=1)

        dq_own, kv_own = against(key_own, value_own, causal)
        dq_old, kv_old = against(key_old, value_old, before)
        query_parts.append(score_scale * (dq_own + dq_old))
        own_sum = own_sum + kv_own
        old_sum = old_sum + kv_old
    query_grad = jnp.concatenate(query_parts, axis=1).astype(jnp.bfloat16)

    quarter = rows // 4
    both = jnp.concatenate([old_sum, own_sum], axis=1).reshape(2, 2, quarter, 4 * HEAD)
    keep = jnp.where(odd, both[:, 1], both[:, 0])
    give = jnp.where(odd, both[:, 0], both[:, 1])
    chip = keep + swap(give, "ffn", 1)
    back = lax.ppermute(chip[:, :, : 2 * HEAD].astype(jnp.bfloat16), "ctx", [(1, 0)])
    total = chip[:, :, 2 * HEAD :] + back.astype(jnp.float32)
    mine = jnp.where(kv_first, total[0], total[1])
    other = swap(jnp.where(kv_first, total[1], total[0]), "ffn", 2)
    first = jnp.where(kv_first, mine, other)
    second = jnp.where(kv_first, other, mine)
    key_grad = score_scale * jnp.concatenate([first[:, :HEAD], second[:, :HEAD]], axis=1)
    value_grad = jnp.concatenate([first[:, HEAD:], second[:, HEAD:]], axis=1)
    return query_grad, key_grad.astype(jnp.bfloat16), value_grad.astype(jnp.bfloat16)


def expert_pair(token_rows, token_grad, gate_probs, expert_ids, w_gate, w_up, w_down):
    experts = EXP_DEV * lax.axis_size("exp")
    slot_count = min(TOK_DEV, TOK_DEV * TOP // experts + 1)
    while slot_count * experts % 8:
        slot_count += 1
    width = token_rows.shape[1]
    first = lax.axis_index("ctx") == 0
    flat_ids = ((expert_ids - lax.axis_index("exp") + experts) % experts).reshape(-1)
    onehot = (flat_ids[:, None] == jnp.arange(experts, dtype=jnp.int32)[None, :]).astype(jnp.int32)
    position = jnp.sum((jnp.cumsum(onehot, axis=0) - 1) * onehot, axis=1)
    target = flat_ids * slot_count + position
    slots = experts * slot_count
    placing = (jnp.arange(slots, dtype=jnp.int32)[:, None] == target[None, :]).astype(jnp.float32)
    token_pick = placing.reshape(slots, token_rows.shape[0], TOP)
    pick_rows = jnp.sum(token_pick, axis=2).astype(jnp.bfloat16)
    slot_gate = jnp.sum(token_pick * gate_probs[None, :, :], axis=(1, 2))
    sent_rows = jnp.dot(pick_rows, token_rows, preferred_element_type=jnp.float32).astype(
        jnp.bfloat16
    )
    sent_grad = (
        jnp.dot(pick_rows, token_grad, preferred_element_type=jnp.float32) * slot_gate[:, None]
    ).astype(jnp.bfloat16)

    def gather(block):
        block = block.reshape(experts, slot_count, width)
        here = [block[0]] + [shift(block[k], "exp", k) for k in range(1, experts)]
        here = jnp.concatenate(here, axis=0)
        far = swap(here, "ffn", 2)
        near = swap(here, "ffn", 1)
        far_near = swap(far, "ffn", 1)

        def order(even, uneven):
            theirs = jnp.where(first, uneven, even)
            mine = jnp.where(first, even, uneven)
            return jnp.concatenate([theirs, mine], axis=0)

        return order(here, near), order(far, far_near)

    x_near, x_far = gather(sent_rows)
    dy_near, dy_far = gather(sent_grad)
    gate_w, up_w, down_w = w_gate[0], w_up[0], w_down[0]

    def summed(partial):
        partial = partial.astype(jnp.bfloat16)
        theirs, mine = partial[:slots], partial[slots:]
        return mine.astype(jnp.float32) + swap(theirs, "ctx", 1).astype(jnp.float32)

    def low_rows(rows_x, rows_dy):
        gate_sum = summed(jnp.dot(rows_x, gate_w, preferred_element_type=jnp.float32))
        up_sum = summed(jnp.dot(rows_x, up_w, preferred_element_type=jnp.float32))
        hidden = summed(
            lax.dot_general(rows_dy, down_w, COLS_COLS, preferred_element_type=jnp.float32)
        )
        gate_mine, up_mine = local_grads(gate_sum, up_sum, hidden)
        gate_low = jnp.concatenate([swap(gate_mine, "ctx", 1), gate_mine], axis=0)
        up_low = jnp.concatenate([swap(up_mine, "ctx", 1), up_mine], axis=0)
        return gate_low, up_low

    def route(gate_low, up_low):
        part = lax.dot_general(
            gate_low, gate_w, COLS_COLS, preferred_element_type=jnp.float32
        ) + lax.dot_general(up_low, up_w, COLS_COLS, preferred_element_type=jnp.float32)
        theirs, mine = part[:slots], part[slots:]
        keep = jnp.where(first, mine, theirs)
        give = jnp.where(first, theirs, mine).astype(jnp.bfloat16)
        return keep + swap(give, "ffn", 1).astype(jnp.float32)

    gate_near, up_near = low_rows(x_near, dy_near)
    gate_far, up_far = low_rows(x_far, dy_far)
    far_sum = route(gate_far, up_far)
    from_far = swap(far_sum.astype(jnp.bfloat16), "ffn", 2)
    total = route(gate_near, up_near) + from_far.astype(jnp.float32)
    total = total.astype(jnp.bfloat16).reshape(experts, slot_count, width)
    back = [total[0]] + [shift(total[k], "exp", -k) for k in range(1, experts)]
    input_grad = lax.dot_general(
        pick_rows, jnp.concatenate(back, axis=0), ROWS_ROWS, preferred_element_type=jnp.float32
    ).astype(jnp.bfloat16)
    rows_x = jnp.concatenate([x_near, x_far], axis=0)
    gate_grad = lax.dot_general(
        rows_x,
        jnp.concatenate([gate_near, gate_far], axis=0),
        ROWS_ROWS,
        preferred_element_type=jnp.float32,
    )
    up_grad = lax.dot_general(
        rows_x,
        jnp.concatenate([up_near, up_far], axis=0),
        ROWS_ROWS,
        preferred_element_type=jnp.float32,
    )
    return (input_grad, gate_grad.astype(jnp.bfloat16)[None], up_grad.astype(jnp.bfloat16)[None])


def local(
    query_rows,
    key_rows,
    value_rows,
    head_output,
    output_grad,
    row_logsumexp,
    token_rows,
    token_grad,
    gate_probs,
    expert_ids,
    w_gate,
    w_up,
    w_down,
):
    kv_heads = key_rows.shape[1] // HEAD
    q_heads = query_rows.shape[1] // HEAD
    paired = lax.axis_size("ctx") == 2 and lax.axis_size("ffn") == 4
    attention = attention_pair if paired and kv_heads == 2 and q_heads == 2 else attention_part
    expert = expert_pair if paired else expert_part
    query_grad, key_grad, value_grad = attention(
        query_rows, key_rows, value_rows, head_output, output_grad, row_logsumexp
    )
    input_grad, gate_grad, up_grad = expert(
        token_rows, token_grad, gate_probs, expert_ids, w_gate, w_up, w_down
    )
    return (query_grad, key_grad, value_grad, input_grad, gate_grad, up_grad)


def solution(mesh):
    return jax.shard_map(
        local,
        mesh=mesh,
        in_specs=(
            P("ctx", ("exp", "ffn")),
            P("ctx", "exp"),
            P("ctx", "exp"),
            P("ctx", ("exp", "ffn")),
            P("ctx", ("exp", "ffn")),
            P(("exp", "ffn"), "ctx"),
            P(("exp", "ffn"), "ctx"),
            P(("exp", "ffn"), "ctx"),
            P(("exp", "ffn"), None),
            P(("exp", "ffn"), None),
            P("exp", "ctx", "ffn"),
            P("exp", "ctx", "ffn"),
            P("exp", "ffn", "ctx"),
        ),
        out_specs=(
            P("ctx", ("exp", "ffn")),
            P(("ctx", "ffn"), "exp"),
            P(("ctx", "ffn"), "exp"),
            P(("exp", "ffn"), "ctx"),
            P("exp", "ctx", "ffn"),
            P("exp", "ctx", "ffn"),
        ),
        check_vma=False,
    )
```

```python
import jax
import jax.numpy as jnp
from jax import lax
from jax.sharding import PartitionSpec as P

QH = 32
KVH = 8
HEAD = 128
TOP = 2
EXP_DEV = 1
TOK_DEV = 64


def attention_part(query_rows, key_rows, value_rows, head_output, output_grad, row_logsumexp):
    tok_ctx = query_rows.shape[0]
    q_heads = query_rows.shape[1] // HEAD
    kv_heads = key_rows.shape[1] // HEAD
    group_size = QH // KVH
    score_scale = HEAD ** (-0.5)
    ffn_index = lax.axis_index("ffn")
    ctx_index = lax.axis_index("ctx")
    query_pos = ctx_index * tok_ctx + jnp.arange(tok_ctx, dtype=jnp.int32)
    product = head_output.astype(jnp.float32) * output_grad.astype(jnp.float32)
    row_delta = jnp.sum(product.reshape(tok_ctx, q_heads, HEAD), axis=2)
    all_keys = tok_ctx * lax.axis_size("ctx")
    contract_rows = (((0,), (0,)), ((), ()))
    contract_cols = (((1,), (1,)), ((), ()))
    start_state = (
        jnp.zeros((tok_ctx, q_heads * HEAD), jnp.float32),
        jnp.zeros((all_keys, kv_heads * HEAD), jnp.float32),
        jnp.zeros((all_keys, kv_heads * HEAD), jnp.float32),
    )
    first_row = jnp.int32(0)
    key_block = lax.all_gather(key_rows, "ctx", axis=0, tiled=True)
    value_block = lax.all_gather(value_rows, "ctx", axis=0, tiled=True)
    key_count = key_block.shape[0]
    key_pos = jnp.arange(key_count, dtype=jnp.int32)
    allowed = key_pos[None, :] <= query_pos[:, None]

    def head_step(head_id, state):
        dq_acc, dk_acc, dv_acc = state
        kv_column = (ffn_index * q_heads + head_id) // group_size * HEAD
        key_head = lax.dynamic_slice_in_dim(key_block, kv_column, HEAD, 1)
        value_head = lax.dynamic_slice_in_dim(value_block, kv_column, HEAD, 1)
        query_head = lax.dynamic_slice_in_dim(query_rows, head_id * HEAD, HEAD, 1)
        grad_head = lax.dynamic_slice_in_dim(output_grad, head_id * HEAD, HEAD, 1)
        lse_row = lax.dynamic_index_in_dim(row_logsumexp, head_id, 0, False)
        delta_row = lax.dynamic_index_in_dim(row_delta, head_id, 1, False)
        scores = (
            lax.dot_general(query_head, key_head, contract_cols, preferred_element_type=jnp.float32)
            * score_scale
        )
        probabilities = jnp.where(allowed, jnp.exp(scores - lse_row[:, None]), 0.0)
        dprob = lax.dot_general(
            grad_head, value_head, contract_cols, preferred_element_type=jnp.float32
        )
        dscores = (probabilities * (dprob - delta_row[:, None])).astype(jnp.bfloat16)
        dq_add = jnp.dot(dscores, key_head, preferred_element_type=jnp.float32)
        old_q = lax.dynamic_slice_in_dim(dq_acc, head_id * HEAD, HEAD, 1)
        dq_acc = lax.dynamic_update_slice_in_dim(dq_acc, old_q + dq_add, head_id * HEAD, 1)
        probs_low = probabilities.astype(jnp.bfloat16)
        value_add = lax.dot_general(
            probs_low, grad_head, contract_rows, preferred_element_type=jnp.float32
        )
        key_add = lax.dot_general(
            dscores, query_head, contract_rows, preferred_element_type=jnp.float32
        )
        old_key = lax.dynamic_slice(dk_acc, (first_row, kv_column), (key_count, HEAD))
        dk_acc = lax.dynamic_update_slice(dk_acc, old_key + key_add, (first_row, kv_column))
        old_value = lax.dynamic_slice(dv_acc, (first_row, kv_column), (key_count, HEAD))
        dv_acc = lax.dynamic_update_slice(dv_acc, old_value + value_add, (first_row, kv_column))
        return (dq_acc, dk_acc, dv_acc)

    finals = lax.fori_loop(0, q_heads, head_step, start_state)
    query_grad = (score_scale * finals[0]).astype(jnp.bfloat16)
    key_sum, value_sum = (
        lax.psum_scatter(finals[1], ("ctx", "ffn"), scatter_dimension=0, tiled=True),
        lax.psum_scatter(finals[2], ("ctx", "ffn"), scatter_dimension=0, tiled=True),
    )
    return (
        query_grad,
        (score_scale * key_sum).astype(jnp.bfloat16),
        value_sum.astype(jnp.bfloat16),
    )


def local_grads(gate_sum, up_sum, hidden):
    sigmoid_gate = jax.nn.sigmoid(gate_sum)
    gate_low = (hidden * up_sum * sigmoid_gate * (1.0 + gate_sum * (1.0 - sigmoid_gate))).astype(
        jnp.bfloat16
    )
    up_low = (hidden * gate_sum * sigmoid_gate).astype(jnp.bfloat16)
    return (gate_low, up_low)


def expert_part(token_rows, token_grad, gate_probs, expert_ids, w_gate, w_up, w_down):
    experts = EXP_DEV * lax.axis_size("exp")
    copies = lax.axis_size("ffn")
    slot_count = min(TOK_DEV, TOK_DEV * TOP // experts + 1)
    tokens_here = token_rows.shape[0]
    feat_width = token_rows.shape[1]
    flat_ids = expert_ids.reshape(-1)
    onehot = (flat_ids[:, None] == jnp.arange(experts, dtype=jnp.int32)[None, :]).astype(jnp.int32)
    position = jnp.sum((jnp.cumsum(onehot, axis=0) - 1) * onehot, axis=1)
    target = flat_ids * slot_count + position
    placing = (
        jnp.arange(experts * slot_count, dtype=jnp.int32)[:, None] == target[None, :]
    ).astype(jnp.float32)
    token_pick = placing.reshape(experts * slot_count, tokens_here, TOP)
    pick_rows = jnp.sum(token_pick, axis=2)
    pick_scaled = jnp.sum(token_pick * gate_probs[None, :, :], axis=2)
    sent_rows = jnp.dot(
        pick_rows.astype(jnp.bfloat16), token_rows, preferred_element_type=jnp.float32
    ).astype(jnp.bfloat16)
    sent_grad = jnp.dot(
        pick_scaled, token_grad.astype(jnp.float32), precision=lax.Precision.HIGHEST
    ).astype(jnp.bfloat16)

    def spread(block):
        widened = jnp.broadcast_to(
            block.reshape(experts, 1, slot_count, feat_width),
            (experts, copies, slot_count, feat_width),
        )
        return widened.reshape(experts * copies * slot_count, feat_width)

    rows_x, rows_dy = (
        lax.all_to_all(spread(sent_rows), ("exp", "ffn"), split_axis=0, concat_axis=0, tiled=True),
        lax.all_to_all(spread(sent_grad), ("exp", "ffn"), split_axis=0, concat_axis=0, tiled=True),
    )
    gate_w = w_gate[0]
    up_w = w_up[0]
    down_w = w_down[0]
    contract_rows = (((0,), (0,)), ((), ()))
    contract_cols = (((1,), (1,)), ((), ()))
    gate_part = jnp.dot(rows_x, gate_w, preferred_element_type=jnp.float32)
    up_part = jnp.dot(rows_x, up_w, preferred_element_type=jnp.float32)
    hidden_part = lax.dot_general(
        rows_dy, down_w, contract_cols, preferred_element_type=jnp.float32
    )
    gate_sum, up_sum, hidden = (
        lax.psum(gate_part.astype(jnp.bfloat16), "ctx").astype(jnp.float32),
        lax.psum(up_part.astype(jnp.bfloat16), "ctx").astype(jnp.float32),
        lax.psum(hidden_part.astype(jnp.bfloat16), "ctx").astype(jnp.float32),
    )
    gate_low, up_low = local_grads(gate_sum, up_sum, hidden)
    gate_grad = lax.dot_general(rows_x, gate_low, contract_rows, preferred_element_type=jnp.float32)
    up_grad = lax.dot_general(rows_x, up_low, contract_rows, preferred_element_type=jnp.float32)
    route_part = lax.dot_general(
        gate_low, gate_w, contract_cols, preferred_element_type=jnp.float32
    ) + lax.dot_general(up_low, up_w, contract_cols, preferred_element_type=jnp.float32)
    returned = lax.all_to_all(
        route_part.astype(jnp.bfloat16), ("exp", "ffn"), split_axis=0, concat_axis=0, tiled=True
    ).astype(route_part.dtype)
    route_grad = jnp.sum(returned.reshape(experts, copies, slot_count, feat_width), axis=1)
    route_grad = route_grad.reshape(experts * slot_count, feat_width)
    input_grad = lax.dot_general(
        pick_rows,
        route_grad,
        contract_rows,
        precision=lax.Precision.HIGHEST,
        preferred_element_type=jnp.float32,
    ).astype(jnp.bfloat16)
    return (input_grad, gate_grad.astype(jnp.bfloat16)[None], up_grad.astype(jnp.bfloat16)[None])


def swap(block, axis, mask):
    size = lax.axis_size(axis)
    return lax.ppermute(block, axis, [(i, i ^ mask) for i in range(size)])


def shift(block, axis, step):
    size = lax.axis_size(axis)
    return lax.ppermute(block, axis, [(i, (i + step) % size) for i in range(size)])


ROWS_ROWS = (((0,), (0,)), ((), ()))
COLS_COLS = (((1,), (1,)), ((), ()))


def attention_pair(query_rows, key_rows, value_rows, head_output, output_grad, row_logsumexp):
    rows = query_rows.shape[0]
    q_heads = query_rows.shape[1] // HEAD
    score_scale = HEAD ** (-0.5)
    ffn_index = lax.axis_index("ffn")
    late = lax.axis_index("ctx") == 1
    kv_first = ffn_index < 2
    odd = ffn_index % 2 == 1
    key_own = jnp.where(kv_first, key_rows[:, :HEAD], key_rows[:, HEAD:])
    value_own = jnp.where(kv_first, value_rows[:, :HEAD], value_rows[:, HEAD:])
    sent = lax.ppermute(jnp.concatenate([key_own, value_own], axis=1), "ctx", [(0, 1)])
    key_old, value_old = sent[:, :HEAD], sent[:, HEAD:]
    product = head_output.astype(jnp.float32) * output_grad.astype(jnp.float32)
    row_delta = jnp.sum(product.reshape(rows, q_heads, HEAD), axis=2)
    place = jnp.arange(rows, dtype=jnp.int32)
    causal = place[None, :] <= place[:, None]
    before = jnp.broadcast_to(late, (rows, rows))
    query_parts = []
    own_sum = old_sum = 0.0
    for head in range(q_heads):
        query_head = query_rows[:, head * HEAD : (head + 1) * HEAD]
        grad_head = output_grad[:, head * HEAD : (head + 1) * HEAD]
        lse = row_logsumexp[head][:, None]
        delta = row_delta[:, head][:, None]

        def against(keys, values, allowed):
            scores = (
                lax.dot_general(query_head, keys, COLS_COLS, preferred_element_type=jnp.float32)
                * score_scale
            )
            probs = jnp.where(allowed, jnp.exp(scores - lse), 0.0)
            dprob = lax.dot_general(
                grad_head, values, COLS_COLS, preferred_element_type=jnp.float32
            )
            dscores = (probs * (dprob - delta)).astype(jnp.bfloat16)
            dq = jnp.dot(dscores, keys, preferred_element_type=jnp.float32)
            dk = lax.dot_general(
                dscores, query_head, ROWS_ROWS, preferred_element_type=jnp.float32
            )
            dv = lax.dot_general(
                probs.astype(jnp.bfloat16), grad_head, ROWS_ROWS, preferred_element_type=jnp.float32
            )
            return dq, jnp.concatenate([dk, dv], axis=1)

        dq_own, kv_own = against(key_own, value_own, causal)
        dq_old, kv_old = against(key_old, value_old, before)
        query_parts.append(score_scale * (dq_own + dq_old))
        own_sum = own_sum + kv_own
        old_sum = old_sum + kv_old
    query_grad = jnp.concatenate(query_parts, axis=1).astype(jnp.bfloat16)

    quarter = rows // 4
    both = jnp.concatenate([old_sum, own_sum], axis=1).reshape(2, 2, quarter, 4 * HEAD)
    keep = jnp.where(odd, both[:, 1], both[:, 0])
    give = jnp.where(odd, both[:, 0], both[:, 1])
    chip = keep + swap(give, "ffn", 1)
    back = lax.ppermute(chip[:, :, : 2 * HEAD].astype(jnp.bfloat16), "ctx", [(1, 0)])
    return query_grad, chip, back


def attention_end(chip, back, kv_first, score_scale):
    total = chip[:, :, 2 * HEAD :] + back.astype(jnp.float32)
    mine = jnp.where(kv_first, total[0], total[1])
    other = swap(jnp.where(kv_first, total[1], total[0]), "ffn", 2)
    first = jnp.where(kv_first, mine, other)
    second = jnp.where(kv_first, other, mine)
    key_grad = score_scale * jnp.concatenate([first[:, :HEAD], second[:, :HEAD]], axis=1)
    value_grad = jnp.concatenate([first[:, HEAD:], second[:, HEAD:]], axis=1)
    return key_grad.astype(jnp.bfloat16), value_grad.astype(jnp.bfloat16)


def after(value, *earlier):
    return lax.optimization_barrier((value,) + earlier)[0]


def expert_pair(chip, back, token_rows, token_grad, gate_probs, expert_ids, w_gate, w_up, w_down):
    experts = EXP_DEV * lax.axis_size("exp")
    slot_count = min(TOK_DEV, TOK_DEV * TOP // experts + 1)
    while slot_count * experts % 8:
        slot_count += 1
    width = token_rows.shape[1]
    first = lax.axis_index("ctx") == 0
    flat_ids = ((expert_ids - lax.axis_index("exp") + experts) % experts).reshape(-1)
    onehot = (flat_ids[:, None] == jnp.arange(experts, dtype=jnp.int32)[None, :]).astype(jnp.int32)
    position = jnp.sum((jnp.cumsum(onehot, axis=0) - 1) * onehot, axis=1)
    target = flat_ids * slot_count + position
    slots = experts * slot_count
    placing = (jnp.arange(slots, dtype=jnp.int32)[:, None] == target[None, :]).astype(jnp.float32)
    token_pick = placing.reshape(slots, token_rows.shape[0], TOP)
    pick_rows = jnp.sum(token_pick, axis=2).astype(jnp.bfloat16)
    slot_gate = jnp.sum(token_pick * gate_probs[None, :, :], axis=(1, 2))
    sent_rows = jnp.dot(pick_rows, token_rows, preferred_element_type=jnp.float32).astype(
        jnp.bfloat16
    )
    sent_grad = (
        jnp.dot(pick_rows, token_grad, preferred_element_type=jnp.float32) * slot_gate[:, None]
    ).astype(jnp.bfloat16)

    def over_experts(block):
        block = block.reshape(experts, slot_count, width)
        return [block[0]] + [shift(block[k], "exp", k) for k in range(1, experts)]

    def order(even, uneven):
        theirs = jnp.where(first, uneven, even)
        mine = jnp.where(first, even, uneven)
        return jnp.concatenate([theirs, mine], axis=0)

    gate_w, up_w, down_w = w_gate[0], w_up[0], w_down[0]

    def halves(rows, weight, dims):
        part = lax.dot_general(rows, weight, dims, preferred_element_type=jnp.float32)
        part = part.astype(jnp.bfloat16)
        return part[slots:], swap(part[:slots], "ctx", 1)

    def added(pair):
        return pair[0].astype(jnp.float32) + pair[1].astype(jnp.float32)

    plain = (((1,), (0,)), ((), ()))
    x_here = jnp.concatenate(over_experts(sent_rows), axis=0)
    x_beside = swap(x_here, "ffn", 1)
    dy_blocks = over_experts(after(sent_grad, x_here))
    x_across = swap(after(x_here, x_beside), "ffn", 2)
    x_near = order(x_here, x_beside)
    gate_pair = halves(x_near, gate_w, plain)
    up_pair = halves(x_near, up_w, plain)
    dy_blocks = [after(block, gate_pair[1], up_pair[0]) for block in dy_blocks]
    dy_here = jnp.concatenate(dy_blocks, axis=0)
    dy_beside = swap(dy_here, "ffn", 1)
    dy_across = swap(after(dy_here, dy_beside), "ffn", 2)
    dy_near = order(dy_here, dy_beside)
    hidden_pair = halves(dy_near, down_w, COLS_COLS)
    x_across = after(x_across, dy_here)
    x_far = order(x_across, swap(x_across, "ffn", 1))
    gate_pair_far = halves(x_far, gate_w, plain)
    up_pair_far = halves(x_far, up_w, plain)
    dy_across = after(dy_across, gate_pair_far[0], up_pair_far[0])
    dy_far = order(dy_across, swap(dy_across, "ffn", 1))
    hidden_pair_far = halves(dy_far, down_w, COLS_COLS)

    gate_pair, up_pair, hidden_pair = (
        (pair[0], after(pair[1], hidden_pair_far[0]))
        for pair in (gate_pair, up_pair, hidden_pair)
    )
    gate_mine, up_mine = local_grads(added(gate_pair), added(up_pair), added(hidden_pair))
    gate_near = jnp.concatenate([swap(gate_mine, "ctx", 1), gate_mine], axis=0)
    gate_mine, up_mine_far = local_grads(
        added(gate_pair_far), added(up_pair_far), added(hidden_pair_far)
    )
    gate_far = jnp.concatenate([swap(gate_mine, "ctx", 1), gate_mine], axis=0)
    up_far = jnp.concatenate([swap(up_mine_far, "ctx", 1), up_mine_far], axis=0)
    up_mine = after(up_mine, gate_near)
    up_near = jnp.concatenate([swap(up_mine, "ctx", 1), up_mine], axis=0)
    back, chip = after(back, gate_near), after(chip, gate_near)
    key_grad, value_grad = attention_end(
        chip, back, lax.axis_index("ffn") < 2, HEAD ** (-0.5)
    )

    def route(gate_low, up_low):
        part = lax.dot_general(
            gate_low, gate_w, COLS_COLS, preferred_element_type=jnp.float32
        ) + lax.dot_general(up_low, up_w, COLS_COLS, preferred_element_type=jnp.float32)
        theirs, mine = part[:slots], part[slots:]
        keep = jnp.where(first, mine, theirs)
        give = jnp.where(first, theirs, mine).astype(jnp.bfloat16)
        return keep + swap(give, "ffn", 1).astype(jnp.float32)

    far_sum = route(gate_far, up_far)
    from_far = swap(far_sum.astype(jnp.bfloat16), "ffn", 2)
    total = route(gate_near, up_near) + from_far.astype(jnp.float32)
    total = total.astype(jnp.bfloat16).reshape(experts, slot_count, width)
    back = [total[0]] + [shift(total[k], "exp", -k) for k in range(1, experts)]
    input_grad = lax.dot_general(
        pick_rows, jnp.concatenate(back, axis=0), ROWS_ROWS, preferred_element_type=jnp.float32
    ).astype(jnp.bfloat16)
    rows_x = jnp.concatenate([x_near, x_far], axis=0)
    gate_grad = lax.dot_general(
        rows_x,
        jnp.concatenate([gate_near, gate_far], axis=0),
        ROWS_ROWS,
        preferred_element_type=jnp.float32,
    )
    up_grad = lax.dot_general(
        rows_x,
        jnp.concatenate([up_near, up_far], axis=0),
        ROWS_ROWS,
        preferred_element_type=jnp.float32,
    )
    return (
        key_grad,
        value_grad,
        input_grad,
        gate_grad.astype(jnp.bfloat16)[None],
        up_grad.astype(jnp.bfloat16)[None],
    )


def local(
    query_rows,
    key_rows,
    value_rows,
    head_output,
    output_grad,
    row_logsumexp,
    token_rows,
    token_grad,
    gate_probs,
    expert_ids,
    w_gate,
    w_up,
    w_down,
):
    kv_heads = key_rows.shape[1] // HEAD
    q_heads = query_rows.shape[1] // HEAD
    paired = lax.axis_size("ctx") == 2 and lax.axis_size("ffn") == 4
    experts_args = (token_rows, token_grad, gate_probs, expert_ids, w_gate, w_up, w_down)
    if paired and kv_heads == 2 and q_heads == 2:
        query_grad, chip, back = attention_pair(
            query_rows, key_rows, value_rows, head_output, output_grad, row_logsumexp
        )
        return (query_grad,) + expert_pair(chip, back, *experts_args)
    query_grad, key_grad, value_grad = attention_part(
        query_rows, key_rows, value_rows, head_output, output_grad, row_logsumexp
    )
    input_grad, gate_grad, up_grad = expert_part(*experts_args)
    return (query_grad, key_grad, value_grad, input_grad, gate_grad, up_grad)


def solution(mesh):
    return jax.shard_map(
        local,
        mesh=mesh,
        in_specs=(
            P("ctx", ("exp", "ffn")),
            P("ctx", "exp"),
            P("ctx", "exp"),
            P("ctx", ("exp", "ffn")),
            P("ctx", ("exp", "ffn")),
            P(("exp", "ffn"), "ctx"),
            P(("exp", "ffn"), "ctx"),
            P(("exp", "ffn"), "ctx"),
            P(("exp", "ffn"), None),
            P(("exp", "ffn"), None),
            P("exp", "ctx", "ffn"),
            P("exp", "ctx", "ffn"),
            P("exp", "ffn", "ctx"),
        ),
        out_specs=(
            P("ctx", ("exp", "ffn")),
            P(("ctx", "ffn"), "exp"),
            P(("ctx", "ffn"), "exp"),
            P(("exp", "ffn"), "ctx"),
            P("exp", "ctx", "ffn"),
            P("exp", "ctx", "ffn"),
        ),
        check_vma=False,
    )
```
